32 devices in a mesh: row: 16 (over z, y, core), col: 2 (over x).
Axes of the slice: x: 2, y: 2, z: 4, core: 2. Of those that a mesh axis runs over, the one named last changes fastest.
Arguments:
- inverse_tiles: bfloat16 [128, 256, 128, 256], P('col', None, 'row'), may hold values from -6 to 6
- factor_panels: bfloat16 [2, 128, 256, 256], P(None, 'row', 'col'), may hold values from -0.0390625 to 0.0390625
- ancestors: int32 [2, 96], replicated, may hold values from 0 to 127, as said below
- valid_flags: int32 [2, 96], replicated, may hold values from 0 to 1, as said below
- block_slot: int32 [128], replicated, may hold values from 0 to 127, each once
Outputs:
- new_panels: float32 [128, 256, 2, 256], P('col', 'row')
The draws below stay inside these ranges and needn't reach their ends.
Inputs may be any that keep to these rules, and one draw needn't show every extreme that they name: `ancestors`: within one supernode's list all 96 entries name different blocks. `valid_flags`: each list's used entries come first; supernode 0's list is used in full, the others in 64 entries or more.
All inputs are finite; a program needn't handle non-finite values.
Results may differ from the reference program's by a relative error of at most 0.0003.
Values may be sent and summed in bfloat16 or wider, within the bound.
A program may use at most 256 MiB of HBM per device.

```python
import jax
import jax.numpy as jnp
from jax import lax

BW = 256
NA = 96
NB = 128
SN = 2
N_ROW = 16


def lists_helper(key):
    base = jax.random.fold_in(key, 11)
    keys = jax.random.split(base, SN)
    block_ids = jax.vmap(lambda single: jax.random.permutation(single, NB)[:NA])(keys).astype(jnp.int32)
    counts = jax.random.randint(jax.random.fold_in(base, 5), (SN,), 2 * NA // 3, NA + 1).astype(jnp.int32)
    counts = counts.at[0].set(NA)
    flags = (jnp.arange(NA, dtype=jnp.int32)[None, :] < counts[:, None]).astype(jnp.int32)
    return (block_ids, flags)


def draw_ancestors(key, part):
    return lists_helper(key)[0]


def draw_valid_flags(key, part):
    return lists_helper(key)[1]


def steps_of(rng, extent, cuts, smallest, top_value):
    factor_of = 1.0
    for dim, blocks in cuts:
        draws = jax.random.uniform(jax.random.fold_in(jax.random.fold_in(rng, 6), dim), (blocks,), jnp.float32, smallest / len(cuts), top_value / len(cuts))
        factor_of = factor_of * jnp.repeat(jnp.exp(draws), extent[dim] // blocks).reshape((-1,) + (1,) * (len(extent) - 1 - dim))
    return factor_of


def noise(stream_key, extent, scale, most, shards=(), held_as=jnp.bfloat16):
    level = steps_of(stream_key, extent, shards, -0.22, 0.18) if shards else 1.0
    entries = jax.random.normal(stream_key, extent, jnp.float32) * scale * level
    return jnp.minimum(jnp.maximum(entries, -most), most).astype(held_as)


def setup_inputs(seed: int = 0) -> dict:
    seeds = jax.random.split(jax.random.key(seed), 6)
    return {
        "inverse_tiles": noise(seeds[0], (NB, BW, NB, BW), 1.0, 6.0, ((0, 2), (2, 16))),
        "factor_panels": noise(seeds[1], (SN, NB, BW, BW), (NA * BW) ** -0.5, 0.0390625, ((1, 16), (2, 2))),
        "ancestors": draw_ancestors(jax.random.fold_in(seeds[5], 71), 0),
        "valid_flags": draw_valid_flags(jax.random.fold_in(seeds[5], 71), 0),
        "block_slot": jax.random.permutation(seeds[4], NB).astype(jnp.int32),
    }


def membership(ancestors, valid_flags, block_slot):
    blocks = jnp.arange(NB, dtype=jnp.int32)
    pick = (ancestors[:, :, None] == blocks[None, None, :]).astype(jnp.int32)
    slots = jnp.sum(pick * block_slot[None, None, :], axis=2)
    hits = (slots[:, :, None] == blocks[None, None, :]) & (valid_flags[:, :, None] == 1)
    return jnp.any(hits, axis=1)


def reference(inverse_tiles, factor_panels, ancestors, valid_flags, block_slot):
    member = membership(ancestors, valid_flags, block_slot)
    masked = jnp.where(member[:, :, None, None], factor_panels, jnp.zeros((), factor_panels.dtype))
    group_len = (NB // N_ROW) * BW
    right = jnp.transpose(masked, (1, 2, 0, 3)).reshape(N_ROW, group_len, SN * BW).astype(jnp.float32)
    left = inverse_tiles.reshape(NB, BW, N_ROW, group_len)

    def one_block(rows):
        grouped = jnp.transpose(rows, (1, 0, 2)).astype(jnp.float32)
        parts = jnp.einsum("grk,gkc->grc", grouped, right)
        return jnp.sum(parts, axis=0)

    product = lax.map(one_block, left).reshape(NB, BW, SN, BW)
    rowmask = jnp.transpose(member)[:, None, :, None]
    return jnp.where(rowmask, -product, jnp.zeros((), product.dtype))
```

```python
import functools

import jax
import jax.numpy as jnp
from jax import lax
from jax.experimental import pallas as pl
from jax.experimental.pallas import tpu as pltpu
from jax.sharding import PartitionSpec as P

MESH_IDS = pl.DeviceIdType.MESH
STEP = 4
RING = 8
TOP = 32766.0


def membership(ancestors, valid_flags, block_slot):
    blocks = jnp.arange(block_slot.shape[0], dtype=jnp.int32)
    pick = (ancestors[:, :, None] == blocks[None, None, :]).astype(jnp.int32)
    slots = jnp.sum(pick * block_slot[None, None, :], axis=2)
    hits = (slots[:, :, None] == blocks[None, None, :]) & (valid_flags[:, :, None] == 1)
    return jnp.any(hits, axis=1)


def panel_product(left, right):
    return jnp.dot(left, right, preferred_element_type=jnp.float32)


def plain_device(inverse_tiles, factor_panels, ancestors, valid_flags, block_slot):
    local_rows = inverse_tiles.shape[0]
    width = inverse_tiles.shape[1]
    local_cols = inverse_tiles.shape[2]
    panel_count = factor_panels.shape[0]
    member = membership(ancestors, valid_flags, block_slot)
    col_start = lax.axis_index("row") * local_cols
    row_start = lax.axis_index("col") * local_rows
    col_member = lax.dynamic_slice_in_dim(member, col_start, local_cols, 1)
    row_member = lax.dynamic_slice_in_dim(member, row_start, local_rows, 1)
    left = inverse_tiles.reshape(local_rows * width, local_cols * width)
    masked_local = jnp.where(
        col_member[:, :, None, None], factor_panels, jnp.zeros((), factor_panels.dtype)
    )
    results = []
    for which in range(panel_count):
        whole = lax.all_gather(masked_local[which], "col", axis=1, tiled=True)
        right = whole.reshape(local_cols * width, width)
        partial_value = panel_product(left, right)
        summed = lax.psum_scatter(
            partial_value.reshape(local_rows, width, width), "row", scatter_dimension=1, tiled=True
        )
        results.append(summed)
    stacked = jnp.stack(results, axis=2)
    rowmask = jnp.transpose(row_member)[:, None, :, None]
    return jnp.where(rowmask, -stacked, jnp.zeros((), jnp.float32))


def fused_kernel(
    dims, order_ref, slot_ref, rowm_ref, colm_ref, panel_ref, left_ref, out_ref,
    left_buf, left_sem, left_mat, right_mat, other_panel, part,
    send_a, recv_a, sscale_a, rscale_a, keep_b, send_b, recv_b, sscale_b, rscale_b,
    keep_c, send_c, recv_c, sscale_c, rscale_c, result,
    panel_sems, a_ss, a_rs, as_ss, as_rs, b_ss, b_rs, bs_ss, bs_rs, c_ss, c_rs, cs_ss, cs_rs,
):
    n_outer, width, n_cols, panels, local_rows, cap, ring = dims
    pairs = local_rows * panels
    tiles = STEP // panels
    lag = (pairs - cap) // STEP
    steps = cap // STEP
    m_steps = pairs // STEP
    chunk = width // (4 * n_outer)
    half = width // 2
    quarter = width // 4
    load_rows = tiles * width * n_cols

    row = lax.axis_index("row")
    col = lax.axis_index("col")
    core = row % 2
    mid = (row // 2) % 2
    outer = row // 4
    sibling = (row + 1 - 2 * core, col)
    across = (row + 2 - 4 * mid, col)
    others = [(((outer + d) % n_outer) * 4 + mid * 2 + core, col) for d in range(1, n_outer)]
    twin = (row, 1 - col)

    barrier = pltpu.get_barrier_semaphore()
    for device in [sibling, across, twin] + others:
        pl.semaphore_signal(barrier, inc=1, device_id=device, device_id_type=MESH_IDS)

    def load(m):
        return pltpu.make_async_copy(
            left_ref.at[pl.ds(pl.multiple_of(m * load_rows, load_rows), load_rows)],
            left_buf.at[m % 3], left_sem.at[m % 3],
        )

    load(0).start()
    load(1).start()
    pl.semaphore_wait(barrier, 2 + n_outer)

    def remote(src, dst, ss, rs, device):
        return pltpu.make_async_remote_copy(
            src_ref=src, dst_ref=dst, send_sem=ss, recv_sem=rs, device_id=device, device_id_type=MESH_IDS
        )

    panel_copy = remote(panel_ref, other_panel, panel_sems.at[0], panel_sems.at[1], twin)
    panel_copy.start()

    deep = width // 2

    def place(source, which_col):
        for b in range(n_cols):
            for s in range(panels):
                block = source[s, b]
                block = jnp.where(colm_ref[s * n_cols + b] > 0, block.astype(jnp.float32), 0.0)
                start = pl.multiple_of(b * width + which_col * deep, deep)
                right_mat[pl.ds(start, deep), pl.ds(s * width, width)] = block.astype(jnp.bfloat16)

    place(panel_ref, col)
    panel_copy.wait()
    place(other_panel, 1 - col)

    def copy_a(t):
        return [
            remote(send_a.at[t % 2], recv_a.at[t % RING], a_ss.at[t % 2], a_rs.at[t % RING], sibling),
            remote(sscale_a.at[t % 2], rscale_a.at[t % RING], as_ss.at[t % 2], as_rs.at[t % RING], sibling),
        ]

    def copy_b(t):
        return [
            remote(send_b.at[t % 2], recv_b.at[t % RING], b_ss.at[t % 2], b_rs.at[t % RING], across),
            remote(sscale_b.at[t % 2], rscale_b.at[t % RING], bs_ss.at[t % 2], bs_rs.at[t % RING], across),
        ]

    def copy_c(t, d):
        return [
            remote(send_c.at[t % 2, d], recv_c.at[t % RING, d], c_ss.at[d, t % 2], c_rs.at[d, t % RING], others[d]),
            remote(sscale_c.at[t % 2], rscale_c.at[t % RING, d], cs_ss.at[d, t % 2], cs_rs.at[d, t % RING], others[d]),
        ]

    def multiply(m):
        @pl.when(m + 2 < m_steps)
        def _():
            load(m + 2).start()

        load(m).wait()
        for g in range(tiles):
            rows = width * n_cols
            band = 32
            for q in range(width // band):
                piece = left_buf[m % 3, pl.ds(g * rows + q * band * n_cols, band * n_cols), :]
                piece = piece.astype(jnp.float32).reshape(band, n_cols, width)
                piece = jnp.swapaxes(piece, 0, 1).astype(jnp.bfloat16)
                for b in range(n_cols):
                    left_mat[
                        pl.ds(g * width + q * band, band), pl.ds(b * width, width)
                    ] = piece[b]
        got = jnp.dot(left_mat[...], right_mat[...], preferred_element_type=jnp.float32)
        base = (m * STEP) % ring
        for g in range(tiles):
            for s in range(panels):
                for o in range(n_outer):
                    for y in range(2):
                        for c in range(2):
                            r0 = g * width + ((o * 2 + y) * 2 + c) * chunk
                            part[base + g * panels + s, c, y, pl.ds(o * chunk, chunk), :] = got[
                                r0:r0 + chunk, s * width:(s + 1) * width
                            ]

    def stage_a(t):
        @pl.when(t >= 2)
        def _():
            for c in copy_a(t):
                c.wait_send()

        top = jnp.zeros((1, width), jnp.float32)
        for k in range(STEP):
            at = order_ref[t * STEP + k]
            for y in range(2):
                value = part[at, 1 - core, y]
                top = jnp.maximum(top, jnp.max(jnp.abs(value), axis=0, keepdims=True))
        top = jnp.maximum(top, 1e-30)
        scale = TOP / top
        for k in range(STEP):
            at = order_ref[t * STEP + k]
            for y in range(2):
                value = part[at, 1 - core, y]
                send_a[t % 2, k, y] = jnp.round(value * scale).astype(jnp.int32).astype(jnp.int16)
        sscale_a[t % 2] = jnp.broadcast_to(top * (1.0 / TOP), (8, width))
        for c in copy_a(t):
            c.start()

    def stage_b(t):
        @pl.when(t >= 2)
        def _():
            for c in copy_b(t):
                c.wait_send()

        for c in copy_a(t):
            c.wait_recv()
        unit = rscale_a[t % RING, pl.ds(0, 1), :]

        def arrived(k, y):
            return unit * recv_a[t % RING, k, y].astype(jnp.int32).astype(jnp.float32)

        top = jnp.zeros((1, width), jnp.float32)
        away = []
        for k in range(STEP):
            at = order_ref[t * STEP + k]
            keep_b[t % 4, k] = part[at, core, mid] + arrived(k, mid)
            value = part[at, core, 1 - mid] + arrived(k, 1 - mid)
            away.append(value)
            top = jnp.maximum(top, jnp.max(jnp.abs(value), axis=0, keepdims=True))
        top = jnp.maximum(top, 1e-30)
        scale = TOP / top
        for k in range(STEP):
            send_b[t % 2, pl.ds(k * quarter, quarter), :] = (
                jnp.round(away[k] * scale).astype(jnp.int32).astype(jnp.int16)
            )
        sscale_b[t % 2] = jnp.broadcast_to(top * (1.0 / TOP), (8, width))
        for c in copy_b(t):
            c.start()

    def stage_c(t):
        @pl.when(t >= 2)
        def _():
            for d in range(n_outer - 1):
                for c in copy_c(t, d):
                    c.wait_send()

        for c in copy_b(t):
            c.wait_recv()
        unit = rscale_b[t % RING, pl.ds(0, 1), :]
        top = jnp.zeros((1, width), jnp.float32)
        for k in range(STEP):
            value = keep_b[t % 4, k] + unit * recv_b[
                t % RING, pl.ds(k * quarter, quarter), :
            ].astype(jnp.int32).astype(jnp.float32)
            keep_c[t % 4, k] = value
            top = jnp.maximum(top, jnp.max(jnp.abs(value), axis=0, keepdims=True))
        top = jnp.maximum(top, 1e-30)
        scale = TOP / top
        for d in range(n_outer - 1):
            goal = (outer + d + 1) % n_outer
            for k in range(STEP):
                value = keep_c[t % 4, k, pl.ds(pl.multiple_of(goal * chunk, chunk), chunk), :]
                send_c[t % 2, d, pl.ds(k * chunk, chunk), :] = (
                    jnp.round(value * scale).astype(jnp.int32).astype(jnp.int16)
                )
        sscale_c[t % 2] = jnp.broadcast_to(top * (1.0 / TOP), (8, width))
        for d in range(n_outer - 1):
            for c in copy_c(t, d):
                c.start()

    def stage_d(t):
        for d in range(n_outer - 1):
            for c in copy_c(t, d):
                c.wait_recv()
        for k in range(STEP):
            value = keep_c[t % 4, k, pl.ds(pl.multiple_of(outer * chunk, chunk), chunk), :]
            for d in range(n_outer - 1):
                unit = rscale_c[t % RING, d, pl.ds(0, 1), :]
                value = value + unit * recv_c[
                    t % RING, d, pl.ds(k * chunk, chunk), :
                ].astype(jnp.int32).astype(jnp.float32)
            result[t * STEP + k] = -value

    def body(it, carry):
        t = it - lag

        @pl.when(it < m_steps)
        def _():
            multiply(it)

        @pl.when((t - 2 >= 0) & (t - 2 < steps))
        def _():
            stage_b(t - 2)

        @pl.when((t - 4 >= 0) & (t - 4 < steps))
        def _():
            stage_c(t - 4)

        @pl.when((t - 6 >= 0) & (t - 6 < steps))
        def _():
            stage_d(t - 6)

        @pl.when((t >= 0) & (t < steps))
        def _():
            stage_a(t)

        return carry

    lax.fori_loop(0, m_steps + 6, body, 0)
    for last in (steps - 2, steps - 1):
        for c in copy_a(last):
            c.wait_send()
        for c in copy_b(last):
            c.wait_send()
        for d in range(n_outer - 1):
            for c in copy_c(last, d):
                c.wait_send()

    def write(i, carry):
        for s in range(panels):
            p = i * panels + s
            value = result[slot_ref[p]]
            out_ref[s, i] = jnp.where(rowm_ref[p] > 0, value, 0.0)
        return carry

    lax.fori_loop(0, local_rows, write, 0)


def fused_call(cap, number, n_row, local_rows, width, n_cols, panels, row_flags, col_flags, left, factor_panels):
    pairs = local_rows * panels
    n_outer = n_row // 4
    chunk = width // n_row
    half, quarter = width // 2, width // 4
    ring = pairs - cap + 4 * STEP
    spot = jnp.arange(pairs, dtype=jnp.int32)
    before = (spot[None, :] < spot[:, None]) & (row_flags[None, :] > 0)
    rank = jnp.sum(before.astype(jnp.int32), axis=1)
    slot = jnp.maximum(rank, spot - (pairs - cap))
    slot_used = jnp.where(row_flags > 0, slot, 0)
    places = jnp.arange(cap, dtype=jnp.int32)
    hit = (slot[None, :] == places[:, None]) & (row_flags[None, :] > 0)
    order = places + jnp.sum(jnp.where(hit, spot[None, :] - places[:, None], 0), axis=1)
    order = order % ring
    load_rows = (STEP // panels) * width * n_cols
    f32, bf16, i16 = jnp.float32, jnp.bfloat16, jnp.int16
    dma = pltpu.SemaphoreType.DMA
    smem = pl.BlockSpec(memory_space=pltpu.SMEM)
    vmem = pl.BlockSpec(memory_space=pltpu.VMEM)
    out = pl.pallas_call(
        functools.partial(fused_kernel, (n_outer, width, n_cols, panels, local_rows, cap, ring)),
        out_shape=jax.ShapeDtypeStruct((panels, local_rows, chunk, width), f32),
        in_specs=[smem, smem, smem, smem, vmem, pl.BlockSpec(memory_space=pl.ANY)],
        out_specs=vmem,
        scratch_shapes=[
            pltpu.VMEM((3, load_rows, width), bf16),
            dma((3,)),
            pltpu.VMEM(((STEP // panels) * width, n_cols * width), bf16),
            pltpu.VMEM((n_cols * width, panels * width), bf16),
            pltpu.VMEM(factor_panels.shape, bf16),
            pltpu.VMEM((ring, 2, 2, quarter, width), f32),
            pltpu.VMEM((2, STEP, 2, quarter, width), i16),
            pltpu.VMEM((RING, STEP, 2, quarter, width), i16),
            pltpu.VMEM((2, 8, width), f32),
            pltpu.VMEM((RING, 8, width), f32),
            pltpu.VMEM((4, STEP, quarter, width), f32),
            pltpu.VMEM((2, STEP * quarter, width), i16),
            pltpu.VMEM((RING, STEP * quarter, width), i16),
            pltpu.VMEM((2, 8, width), f32),
            pltpu.VMEM((RING, 8, width), f32),
            pltpu.VMEM((4, STEP, quarter, width), f32),
            pltpu.VMEM((2, n_outer - 1, STEP * chunk, width), i16),
            pltpu.VMEM((RING, n_outer - 1, STEP * chunk, width), i16),
            pltpu.VMEM((2, 8, width), f32),
            pltpu.VMEM((RING, n_outer - 1, 8, width), f32),
            pltpu.VMEM((cap, chunk, width), f32),
            dma((2,)),
            dma((2,)), dma((RING,)), dma((2,)), dma((RING,)),
            dma((2,)), dma((RING,)), dma((2,)), dma((RING,)),
            dma((n_outer - 1, 2)), dma((n_outer - 1, RING)),
            dma((n_outer - 1, 2)), dma((n_outer - 1, RING)),
        ],
        compiler_params=pltpu.CompilerParams(
            collective_id=number, has_side_effects=True, vmem_limit_bytes=56 * 1024 * 1024
        ),
    )(order, slot_used, row_flags, col_flags, factor_panels, left)
    return out


def per_device(n_row, inverse_tiles, factor_panels, ancestors, valid_flags, block_slot):
    local_rows, width, n_cols, _ = inverse_tiles.shape
    panels = factor_panels.shape[0]
    pairs = local_rows * panels
    member = membership(ancestors, valid_flags, block_slot)
    halves = member.reshape(panels, -1, local_rows)
    count = jnp.max(jnp.sum(halves.astype(jnp.int32), axis=(0, 2)))
    col_start = lax.axis_index("row") * n_cols
    row_start = lax.axis_index("col") * local_rows
    col_flags = lax.dynamic_slice_in_dim(member, col_start, n_cols, 1).astype(jnp.int32).reshape(-1)
    row_flags = jnp.transpose(
        lax.dynamic_slice_in_dim(member, row_start, local_rows, 1)
    ).astype(jnp.int32).reshape(-1)
    left = inverse_tiles.reshape(local_rows * width * n_cols, width)
    caps = CAPS(pairs)
    calls = [
        functools.partial(fused_call, cap, k, n_row, local_rows, width, n_cols, panels)
        for k, cap in enumerate(caps)
    ]
    args = (row_flags, col_flags, left, factor_panels)
    if len(calls) == 1:
        out = calls[0](*args)
    else:
        which = sum((count > cap).astype(jnp.int32) for cap in caps[:-1])
        out = lax.switch(which, calls, *args)
    return jnp.transpose(out, (1, 2, 0, 3))


def CAPS(pairs):
    return [pairs]


def fits(mesh):
    n_row, n_col = mesh.shape["row"], mesh.shape["col"]
    return n_col == 2 and n_row % 4 == 0 and n_row <= 16


def solution(mesh):
    body = functools.partial(per_device, mesh.shape["row"]) if fits(mesh) else plain_device
    return jax.shard_map(
        body,
        mesh=mesh,
        in_specs=(P("col", None, "row", None), P(None, "row", "col", None), P(), P(), P()),
        out_specs=P("col", "row", None, None),
        check_vma=False,
    )
```
